32 devices in a mesh: band: 8 (over y, x, core), grid: 4 (over z).
Axes of the slice: x: 2, y: 2, z: 4, core: 2. Of those that a mesh axis runs over, the one named last changes fastest.
Arguments:
- orbitals: float32 [16, 96, 9216], P('band', 'grid'), may hold values from -6 to 6
Outputs:
- exchange_images: float32 [16, 96, 9216], P('band', 'grid')
- projection: float32 [16, 2], P('band')
The draws below stay inside these ranges and needn't reach their ends.
All inputs are finite; a program needn't handle non-finite values.
Results may differ from the reference program's by a relative error of at most 0.0003.
Values sent between devices are 32-bit elements; how exact they have to be, the bound alone decides.
A program may use at most 64 MiB of HBM per device.

```python
import math
import jax
import jax.numpy as jnp
from jax import lax

G = 96
B_DEV = 2
STEPS = 2
BANDS = 16
N_BAND = 8


def level_of(own_key, dims, shards, low, largest):
    loudness, own = 1.0, jax.random.fold_in(own_key, 6)
    for axis_at, parts in shards:
        steps = jnp.exp(jax.random.uniform(jax.random.fold_in(own, axis_at), (parts,), jnp.float32, low / len(shards), largest / len(shards)))
        loudness = loudness * jnp.repeat(steps, dims[axis_at] // parts).reshape([-1 if axis == axis_at else 1 for axis in range(len(dims))])
    return loudness


def noise(own_key, extent, width, reach, shards=(), kind=jnp.bfloat16):
    factor_of = level_of(own_key, extent, shards, -0.22, 0.18) if shards else 1.0
    entries = jax.random.normal(own_key, extent, jnp.float32) * width * factor_of
    return jnp.minimum(jnp.maximum(entries, -reach), reach).astype(kind)


def setup_inputs(seed: int = 0) -> dict:
    key_of = jax.random.split(jax.random.key(seed), 2)
    return {
        "orbitals": noise(key_of[0], (BANDS, G, G * G), 1.0, 6.0, ((0, 8), (1, 4)), jnp.float32),
    }


cell_edge = 41.05
mixing = 0.25


def coulomb_kernel():
    frequency = jnp.arange(G, dtype=jnp.int32)
    wrapped = jnp.minimum(frequency, G - frequency)
    halfway = jnp.arange(G // 2 + 1, dtype=jnp.int32)
    squared = (wrapped[:, None, None] * wrapped[:, None, None]
               + wrapped[None, :, None] * wrapped[None, :, None]
               + halfway[None, None, :] * halfway[None, None, :])
    scale = cell_edge * cell_edge / math.pi
    return jnp.where(squared > 0, scale / jnp.maximum(squared, 1).astype(jnp.float32), jnp.float32(0.0))


def poisson(density, kernel):
    spectrum = jnp.fft.rfftn(density, axes=(-3, -2, -1))
    return jnp.fft.irfftn(spectrum * kernel, s=(G, G, G), axes=(-3, -2, -1))


def reference(orbitals):
    kernel = coulomb_kernel()
    blocks = orbitals.reshape(N_BAND, B_DEV, G, G, G)

    def per_block(block_index):
        home_block = blocks[block_index]
        own_sum = jnp.zeros_like(home_block)
        returned = []
        for hop_index in range(1, STEPS + 1):
            visitor = blocks[(block_index - hop_index) % N_BAND]
            potential = poisson(home_block[:, None] * visitor[None], kernel)
            own_sum = own_sum - mixing * jnp.sum(potential * visitor[None], axis=1)
            returned.append(-mixing * jnp.sum(potential * home_block[:, None], axis=0))
        return own_sum, jnp.stack(returned)

    own_all, back_all = lax.map(per_block, jnp.arange(N_BAND, dtype=jnp.int32))
    images = own_all
    for hop_index in range(1, STEPS + 1):
        images = images + jnp.roll(back_all[:, hop_index - 1], -hop_index, axis=0)
    intersection = jnp.einsum("pir,pjr->pij", blocks.reshape(N_BAND, B_DEV, G * G * G),
                         images.reshape(N_BAND, B_DEV, G * G * G),
                         precision=lax.Precision.HIGHEST) / float(G * G * G)
    return images.reshape(BANDS, G, G * G), intersection.reshape(BANDS, B_DEV)
```

```python
import math

import jax
import jax.numpy as jnp
from jax import lax
from jax.sharding import PartitionSpec as P

G = 96
STEPS = 2


cell_edge = 41.05
mixing = 0.25
highest = lax.Precision.HIGHEST
split = lax.Precision.HIGH


def passed_along(x, axis, by):
    length = lax.axis_size(axis)
    return lax.ppermute(x, axis, [(i, (i + by) % length) for i in range(length)])


def cas_table(length):
    position = jnp.arange(length, dtype=jnp.int32)
    phase = position[:, None] * position[None, :] % length
    angle = phase.astype(jnp.float32) * (2.0 * math.pi / length)
    return jnp.cos(angle) + jnp.sin(angle)


def folded_square(values, length):
    wrapped = jnp.minimum(values, length - values)
    return wrapped * wrapped


def shards(orbitals):
    band_count = orbitals.shape[0]
    slab_width = orbitals.shape[1]
    grid_count = lax.axis_size("grid")
    column_width = G // grid_count
    pairs = band_count * band_count
    lanes = pairs * G
    cas_values = cas_table(G)
    lane_table = jnp.kron(jnp.eye(pairs, dtype=jnp.float32), cas_values)
    frequency = jnp.arange(G, dtype=jnp.int32)
    my_columns = lax.axis_index("grid") * column_width + jnp.arange(column_width, dtype=jnp.int32)
    squared = (
        folded_square(frequency, G)[:, None, None]
        + folded_square(my_columns, G)[None, :, None]
        + folded_square(frequency, G)[None, None, :]
    )
    coulomb = cell_edge * cell_edge / math.pi / float(G * G * G)
    kernel = jnp.where(
        squared > 0, coulomb / jnp.maximum(squared, 1).astype(jnp.float32), jnp.float32(0.0)
    )
    kernel = jnp.tile(kernel, (1, 1, pairs))

    def forward(density):
        volume = jnp.einsum("xyl,lm->xym", density, lane_table, precision=split)
        volume = jnp.einsum("xym,dy->xdm", volume, cas_values, precision=split)
        return volume.reshape(slab_width, grid_count, column_width, lanes).transpose(1, 0, 2, 3)

    def column_solve(parts):
        volume = parts.reshape(G, column_width, lanes)
        spectrum = jnp.einsum("kx,xyl->kyl", cas_values, volume, precision=split) * kernel
        potential = jnp.einsum("xk,kyl->xyl", cas_values, spectrum, precision=split)
        return potential.reshape(parts.shape)

    def backward(parts):
        volume = parts.transpose(1, 0, 2, 3).reshape(slab_width, G, lanes)
        volume = jnp.einsum("xdm,yd->xym", volume, cas_values, precision=split)
        return jnp.einsum("xym,ml->xyl", volume, lane_table, precision=split)

    def exchange(parts):
        return lax.all_to_all(parts, "grid", split_axis=0, concat_axis=0, tiled=True)

    cubes = orbitals.reshape(band_count, slab_width, G, G)
    own = [cubes[i] for i in range(band_count)]
    wide_own = jnp.concatenate([own[i] for i in range(band_count) for _ in range(band_count)], axis=2)

    visitors = []
    current = jnp.concatenate(own, axis=2)
    for hop_index in range(STEPS):
        current = passed_along(current, "band", 1)
        visitors.append(current)
    sent = [
        exchange(forward(wide_own * jnp.concatenate([visitor] * band_count, axis=2)))
        for visitor in visitors
    ]
    returned = [exchange(column_solve(parts)) for parts in sent]
    own_sum = [0.0] * band_count
    returned_parts = []
    for parts, visitor in zip(returned, visitors):
        potential = backward(parts)
        to_own = potential * jnp.concatenate([visitor] * band_count, axis=2)
        to_visitor = potential * wide_own
        back = []
        for j in range(band_count):
            total = 0.0
            for i in range(band_count):
                at = (i * band_count + j) * G
                total = total + to_visitor[:, :, at:at + G]
            back.append(total)
        for i in range(band_count):
            for j in range(band_count):
                at = (i * band_count + j) * G
                own_sum[i] = own_sum[i] + to_own[:, :, at:at + G]
        returned_parts.append(jnp.concatenate(back, axis=2))
    carried = returned_parts[STEPS - 1]
    for hop_index in reversed(range(STEPS)):
        carried = passed_along(carried, "band", -1)
        if hop_index:
            carried = carried + returned_parts[hop_index - 1]
    images = -mixing * (
        jnp.stack(own_sum) + jnp.stack([carried[:, :, i * G:(i + 1) * G] for i in range(band_count)])
    )
    partial_value = jnp.einsum(
        "ixyz,jxyz->ij", cubes, images, precision=highest
    ) / float(G * G * G)
    intersection = lax.psum(partial_value, "grid")
    return (images.reshape(orbitals.shape), intersection)


def solution(mesh):
    return jax.shard_map(
        shards,
        mesh=mesh,
        in_specs=(P("band", "grid", None),),
        out_specs=(P("band", "grid", None), P("band", None)),
        check_vma=False,
    )
```

```python
import math

import jax
import jax.numpy as jnp
from jax import lax
from jax.sharding import PartitionSpec as P

G = 96
STEPS = 2


cell_edge = 41.05
mixing = 0.25
split = lax.Precision.HIGH


def passed_along(x, axis, by):
    length = lax.axis_size(axis)
    return lax.ppermute(x, axis, [(i, (i + by) % length) for i in range(length)])


def cas_table(length):
    position = jnp.arange(length, dtype=jnp.int32)
    phase = position[:, None] * position[None, :] % length
    angle = phase.astype(jnp.float32) * (2.0 * math.pi / length)
    return jnp.cos(angle) + jnp.sin(angle)


def folded_square(values, length):
    wrapped = jnp.minimum(values, length - values)
    return wrapped * wrapped


def shards(orbitals):
    band_count = orbitals.shape[0]
    slab_width = orbitals.shape[1]
    grid_count = lax.axis_size("grid")
    column_width = G // grid_count
    pairs = band_count * band_count
    lanes = pairs * G
    cas_values = cas_table(G)
    lane_table = jnp.kron(jnp.eye(pairs, dtype=jnp.float32), cas_values)
    frequency = jnp.arange(G, dtype=jnp.int32)
    my_columns = lax.axis_index("grid") * column_width + jnp.arange(column_width, dtype=jnp.int32)
    squared = (
        folded_square(frequency, G)[:, None, None]
        + folded_square(my_columns, G)[None, :, None]
        + folded_square(frequency, G)[None, None, :]
    )
    coulomb = cell_edge * cell_edge / math.pi / float(G * G * G)
    kernel = jnp.where(
        squared > 0, coulomb / jnp.maximum(squared, 1).astype(jnp.float32), jnp.float32(0.0)
    )
    kernel = jnp.tile(kernel, (1, 1, pairs))

    def forward(density):
        volume = jnp.einsum("xyl,lm->xym", density, lane_table, precision=split)
        volume = jnp.einsum("xym,dy->xdm", volume, cas_values, precision=split)
        return volume.reshape(density.shape[0], grid_count, column_width, lanes).transpose(1, 0, 2, 3)

    def column_solve(parts):
        volume = parts.reshape(G, column_width, lanes)
        spectrum = jnp.einsum("kx,xyl->kyl", cas_values, volume, precision=split) * kernel
        potential = jnp.einsum("xk,kyl->xyl", cas_values, spectrum, precision=split)
        return potential.reshape(parts.shape)

    def backward(parts):
        volume = parts.transpose(1, 0, 2, 3).reshape(slab_width, G, lanes)
        volume = jnp.einsum("xdm,yd->xym", volume, cas_values, precision=split)
        return jnp.einsum("xym,ml->xyl", volume, lane_table, precision=split)

    def exchange(parts):
        return lax.all_to_all(parts, "grid", split_axis=0, concat_axis=0, tiled=True)

    def lanes_of(block):
        rows = block.shape[1]
        cubes = block.reshape(band_count, rows, G, G)
        return [cubes[i] for i in range(band_count)]

    def repeated(bands):
        return jnp.concatenate([band for band in bands for _ in range(band_count)], axis=2)

    def tiled(bands):
        return jnp.concatenate(list(bands) * band_count, axis=2)

    head = slab_width // 3
    bounds = [(0, head), (head, slab_width)]
    raw = [orbitals[:, low:high] for low, high in bounds]
    wide_own = [repeated(lanes_of(part)) for part in raw]

    wide_visitors = []
    for hop_index in range(STEPS):
        raw = [passed_along(part, "band", 1) for part in raw]
        wide_visitors.append([tiled(lanes_of(part)) for part in raw])

    def joined(blocks):
        return jnp.concatenate(blocks, axis=1)

    sent = []
    for hop_index in range(STEPS):
        ready = [forward(o * v) for o, v in zip(wide_own, wide_visitors[hop_index])]
        if hop_index == 0:
            sent.append(joined([exchange(part) for part in ready]))
        else:
            sent.append(exchange(joined(ready)))
    solved = [column_solve(parts) for parts in sent]
    wide_own = jnp.concatenate(wide_own, axis=0)
    wide_visitors = [jnp.concatenate(parts, axis=0) for parts in wide_visitors]

    def band_sums(wide, by_own):
        out = []
        for kept in range(band_count):
            total = 0.0
            for other in range(band_count):
                pair = kept * band_count + other if by_own else other * band_count + kept
                total = total + wide[:, :, pair * G:(pair + 1) * G]
            out.append(total)
        return out

    def overlaps(wide_left, by_own, right):
        rows = []
        for a in range(band_count):
            at = (a * band_count if by_own else a) * G
            left = wide_left[:, :, at:at + G]
            rows.append(jnp.stack([jnp.sum(left * right[b]) for b in range(band_count)]))
        return jnp.stack(rows)

    own_sum = None
    own_overlap = 0.0
    carried = None
    carried_overlap = None
    half = G // 2
    held_back = None
    for hop_index in reversed(range(STEPS)):
        parts = solved[hop_index]
        if held_back is not None:
            parts, held_back = lax.optimization_barrier((parts, held_back))
        held_back = exchange(parts)
        potential = backward(held_back)
        to_own = band_sums(potential * wide_visitors[hop_index], True)
        back = band_sums(potential * wide_own, False)
        own_overlap = own_overlap + overlaps(wide_own, True, to_own)
        back_overlap = overlaps(wide_visitors[hop_index], False, back)
        own_sum = to_own if own_sum is None else [x + y for x, y in zip(own_sum, to_own)]
        back = jnp.concatenate(back, axis=2)
        back = jnp.concatenate([back[:, :half], back[:, half:]], axis=2)
        carried = passed_along(back if carried is None else carried + back, "band", -1)
        if carried_overlap is not None:
            back_overlap = back_overlap + carried_overlap
        carried_overlap = passed_along(back_overlap, "band", -1)
    intersection = lax.psum((own_overlap + carried_overlap) * (-mixing / float(G * G * G)), "grid")
    width = band_count * G
    carried = jnp.concatenate([carried[:, :, :width], carried[:, :, width:]], axis=1)
    images = -mixing * jnp.stack(
        [own_sum[i] + carried[:, :, i * G:(i + 1) * G] for i in range(band_count)]
    )
    return (images.reshape(orbitals.shape), intersection)


def solution(mesh):
    return jax.shard_map(
        shards,
        mesh=mesh,
        in_specs=(P("band", "grid", None),),
        out_specs=(P("band", "grid", None), P("band", None)),
        check_vma=False,
    )
```

```python
import math

import jax
import jax.numpy as jnp
from jax import lax
from jax.sharding import PartitionSpec as P

G = 96
STEPS = 2


cell_edge = 41.05
mixing = 0.25
split = lax.Precision.HIGH


def passed_along(x, axis, by):
    length = lax.axis_size(axis)
    return lax.ppermute(x, axis, [(i, (i + by) % length) for i in range(length)])


def cas_table(length):
    position = jnp.arange(length, dtype=jnp.int32)
    phase = position[:, None] * position[None, :] % length
    angle = phase.astype(jnp.float32) * (2.0 * math.pi / length)
    return jnp.cos(angle) + jnp.sin(angle)


def folded_square(values, length):
    wrapped = jnp.minimum(values, length - values)
    return wrapped * wrapped


def shards(orbitals):
    band_count = orbitals.shape[0]
    slab_width = orbitals.shape[1]
    grid_count = lax.axis_size("grid")
    column_width = G // grid_count
    pairs = band_count * band_count
    lanes = pairs * G
    cas_values = cas_table(G)
    lane_table = jnp.kron(jnp.eye(pairs, dtype=jnp.float32), cas_values)
    frequency = jnp.arange(G, dtype=jnp.int32)
    my_columns = lax.axis_index("grid") * column_width + jnp.arange(column_width, dtype=jnp.int32)
    squared = (
        folded_square(frequency, G)[:, None, None]
        + folded_square(my_columns, G)[None, :, None]
        + folded_square(frequency, G)[None, None, :]
    )
    coulomb = cell_edge * cell_edge / math.pi / float(G * G * G)
    kernel = jnp.where(
        squared > 0, coulomb / jnp.maximum(squared, 1).astype(jnp.float32), jnp.float32(0.0)
    )
    kernel = jnp.tile(kernel, (1, 1, pairs))

    def forward(density):
        volume = jnp.einsum("xyl,lm->xym", density, lane_table, precision=split)
        volume = jnp.einsum("xym,dy->xdm", volume, cas_values, precision=split)
        return volume.reshape(density.shape[0], grid_count, column_width, lanes).transpose(1, 0, 2, 3)

    def column_solve(parts):
        volume = parts.reshape(G, column_width, lanes)
        spectrum = jnp.einsum("kx,xyl->kyl", cas_values, volume, precision=split) * kernel
        potential = jnp.einsum("xk,kyl->xyl", cas_values, spectrum, precision=split)
        return potential.reshape(parts.shape)

    def backward(parts):
        volume = parts.transpose(1, 0, 2, 3).reshape(slab_width, G, lanes)
        volume = jnp.einsum("xdm,yd->xym", volume, cas_values, precision=split)
        return jnp.einsum("xym,ml->xyl", volume, lane_table, precision=split)

    def exchange(parts):
        return lax.all_to_all(parts, "grid", split_axis=0, concat_axis=0, tiled=True)

    def lanes_of(block):
        rows = block.shape[1]
        cubes = block.reshape(band_count, rows, G, G)
        return [cubes[i] for i in range(band_count)]

    def repeated(bands):
        return jnp.concatenate([band for band in bands for _ in range(band_count)], axis=2)

    def tiled(bands):
        return jnp.concatenate(list(bands) * band_count, axis=2)

    head = slab_width // 3
    bounds = [(0, head), (head, slab_width)]
    raw = [orbitals[:, low:high] for low, high in bounds]
    wide_own = [repeated(lanes_of(part)) for part in raw]

    wide_visitors = []
    for hop_index in range(STEPS):
        raw = [passed_along(part, "band", 1) for part in raw]
        wide_visitors.append([tiled(lanes_of(part)) for part in raw])

    def joined(blocks):
        return jnp.concatenate(blocks, axis=1)

    sent = []
    for hop_index in range(STEPS):
        ready = [forward(o * v) for o, v in zip(wide_own, wide_visitors[hop_index])]
        if hop_index == 0:
            sent.append(joined([exchange(part) for part in ready]))
        else:
            sent.append(exchange(joined(ready)))
    solved = [column_solve(parts) for parts in sent]
    wide_own = jnp.concatenate(wide_own, axis=0)
    wide_visitors = [jnp.concatenate(parts, axis=0) for parts in wide_visitors]

    def band_sums(wide, by_own):
        out = []
        for kept in range(band_count):
            total = 0.0
            for other in range(band_count):
                pair = kept * band_count + other if by_own else other * band_count + kept
                total = total + wide[:, :, pair * G:(pair + 1) * G]
            out.append(total)
        return out

    def overlaps(wide_left, by_own, right):
        rows = []
        for a in range(band_count):
            at = (a * band_count if by_own else a) * G
            left = wide_left[:, :, at:at + G]
            rows.append(jnp.stack([jnp.sum(left * right[b]) for b in range(band_count)]))
        return jnp.stack(rows)

    own_sum = None
    own_overlap = 0.0
    carried = None
    carried_overlap = None
    half = G // 2
    held_back = None
    for hop_index in reversed(range(STEPS)):
        parts = solved[hop_index]
        if held_back is not None:
            parts, held_back = lax.optimization_barrier((parts, held_back))
        held_back = exchange(parts)
        potential = backward(held_back)
        to_own = band_sums(potential * wide_visitors[hop_index], True)
        back = band_sums(potential * wide_own, False)
        own_overlap = own_overlap + overlaps(wide_own, True, to_own)
        back_overlap = overlaps(wide_visitors[hop_index], False, back)
        back, own_overlap, back_overlap = lax.optimization_barrier((back, own_overlap, back_overlap))
        own_sum = to_own if own_sum is None else [x + y for x, y in zip(own_sum, to_own)]
        back = jnp.concatenate(back, axis=2)
        back = jnp.concatenate([back[:, :half], back[:, half:]], axis=2)
        carried = passed_along(back if carried is None else carried + back, "band", -1)
        if carried_overlap is not None:
            back_overlap = back_overlap + carried_overlap
        carried_overlap = passed_along(back_overlap, "band", -1)
    intersection = lax.psum((own_overlap + carried_overlap) * (-mixing / float(G * G * G)), "grid")
    width = band_count * G
    carried = jnp.concatenate([carried[:, :, :width], carried[:, :, width:]], axis=1)
    images = -mixing * jnp.stack(
        [own_sum[i] + carried[:, :, i * G:(i + 1) * G] for i in range(band_count)]
    )
    return (images.reshape(orbitals.shape), intersection)


def solution(mesh):
    return jax.shard_map(
        shards,
        mesh=mesh,
        in_specs=(P("band", "grid", None),),
        out_specs=(P("band", "grid", None), P("band", None)),
        check_vma=False,
    )
```

```python
import math

import jax
import jax.numpy as jnp
from jax import lax
from jax.sharding import PartitionSpec as P

G = 96
STEPS = 2


cell_edge = 41.05
mixing = 0.25
split = lax.Precision.HIGH


def passed_along(x, axis, by):
    length = lax.axis_size(axis)
    return lax.ppermute(x, axis, [(i, (i + by) % length) for i in range(length)])


def cas_table(length):
    position = jnp.arange(length, dtype=jnp.int32)
    phase = position[:, None] * position[None, :] % length
    angle = phase.astype(jnp.float32) * (2.0 * math.pi / length)
    return jnp.cos(angle) + jnp.sin(angle)


def folded_square(values, length):
    wrapped = jnp.minimum(values, length - values)
    return wrapped * wrapped


def shards(orbitals):
    band_count = orbitals.shape[0]
    slab_width = orbitals.shape[1]
    grid_count = lax.axis_size("grid")
    column_width = G // grid_count
    pairs = band_count * band_count
    lanes = pairs * G
    cas_values = cas_table(G)
    lane_table = jnp.kron(jnp.eye(pairs, dtype=jnp.float32), cas_values)
    frequency = jnp.arange(G, dtype=jnp.int32)
    my_columns = lax.axis_index("grid") * column_width + jnp.arange(column_width, dtype=jnp.int32)
    squared = (
        folded_square(frequency, G)[:, None, None]
        + folded_square(my_columns, G)[None, :, None]
        + folded_square(frequency, G)[None, None, :]
    )
    coulomb = cell_edge * cell_edge / math.pi / float(G * G * G)
    kernel = jnp.where(
        squared > 0, coulomb / jnp.maximum(squared, 1).astype(jnp.float32), jnp.float32(0.0)
    )
    kernel = jnp.tile(kernel, (1, 1, pairs))

    def forward(density):
        volume = jnp.einsum("xyl,lm->xym", density, lane_table, precision=split)
        volume = jnp.einsum("xym,dy->xdm", volume, cas_values, precision=split)
        return volume.reshape(density.shape[0], grid_count, column_width, lanes).transpose(1, 0, 2, 3)

    def column_solve(parts):
        volume = parts.reshape(G, column_width, lanes)
        spectrum = jnp.einsum("kx,xyl->kyl", cas_values, volume, precision=split) * kernel
        potential = jnp.einsum("xk,kyl->xyl", cas_values, spectrum, precision=split)
        return potential.reshape(parts.shape)

    def backward(parts):
        volume = parts.transpose(1, 0, 2, 3).reshape(slab_width, G, lanes)
        volume = jnp.einsum("xdm,yd->xym", volume, cas_values, precision=split)
        return jnp.einsum("xym,ml->xyl", volume, lane_table, precision=split)

    def exchange(parts):
        return lax.all_to_all(parts, "grid", split_axis=0, concat_axis=0, tiled=True)

    def lanes_of(block):
        rows = block.shape[1]
        cubes = block.reshape(band_count, rows, G, G)
        return [cubes[i] for i in range(band_count)]

    def repeated(bands):
        return jnp.concatenate([band for band in bands for _ in range(band_count)], axis=2)

    def tiled(bands):
        return jnp.concatenate(list(bands) * band_count, axis=2)

    head = slab_width // 3
    bounds = [(0, head), (head, slab_width)]
    raw = [orbitals[:, low:high] for low, high in bounds]
    wide_own = [repeated(lanes_of(part)) for part in raw]

    wide_visitors = []
    for hop_index in range(STEPS):
        raw = [passed_along(part, "band", 1) for part in raw]
        wide_visitors.append([tiled(lanes_of(part)) for part in raw])

    def joined(blocks):
        return jnp.concatenate(blocks, axis=1)

    sent = []
    for hop_index in range(STEPS):
        ready = [forward(o * v) for o, v in zip(wide_own, wide_visitors[hop_index])]
        if hop_index == 0:
            sent.append(joined([exchange(part) for part in ready]))
        else:
            sent.append(exchange(joined(ready)))
    solved = [column_solve(parts) for parts in sent]
    wide_own = jnp.concatenate(wide_own, axis=0)
    wide_visitors = [jnp.concatenate(parts, axis=0) for parts in wide_visitors]

    def band_sums(wide, by_own):
        out = []
        for kept in range(band_count):
            total = 0.0
            for other in range(band_count):
                pair = kept * band_count + other if by_own else other * band_count + kept
                total = total + wide[:, :, pair * G:(pair + 1) * G]
            out.append(total)
        return out

    def overlaps(wide_left, by_own, right):
        rows = []
        for a in range(band_count):
            at = (a * band_count if by_own else a) * G
            left = wide_left[:, :, at:at + G]
            rows.append(jnp.stack([jnp.sum(left * right[b]) for b in range(band_count)]))
        return jnp.stack(rows)

    own_sum = None
    own_overlap = 0.0
    carried = None
    carried_overlap = None
    half = G // 2
    for hop_index in reversed(range(STEPS)):
        parts = solved[hop_index]
        potential = backward(exchange(parts))
        to_own = band_sums(potential * wide_visitors[hop_index], True)
        back = band_sums(potential * wide_own, False)
        own_overlap = own_overlap + overlaps(wide_own, True, to_own)
        back_overlap = overlaps(wide_visitors[hop_index], False, back)
        own_sum = to_own if own_sum is None else [x + y for x, y in zip(own_sum, to_own)]
        back = jnp.concatenate(back, axis=2)
        back = jnp.concatenate([back[:, :half], back[:, half:]], axis=2)
        carried = passed_along(back if carried is None else carried + back, "band", -1)
        if carried_overlap is not None:
            back_overlap = back_overlap + carried_overlap
        carried_overlap = passed_along(back_overlap, "band", -1)
    intersection = lax.psum((own_overlap + carried_overlap) * (-mixing / float(G * G * G)), "grid")
    width = band_count * G
    carried = jnp.concatenate([carried[:, :, :width], carried[:, :, width:]], axis=1)
    images = -mixing * jnp.stack(
        [own_sum[i] + carried[:, :, i * G:(i + 1) * G] for i in range(band_count)]
    )
    return (images.reshape(orbitals.shape), intersection)


def solution(mesh):
    return jax.shard_map(
        shards,
        mesh=mesh,
        in_specs=(P("band", "grid", None),),
        out_specs=(P("band", "grid", None), P("band", None)),
        check_vma=False,
    )
```
